32 devices in a mesh: dp: 4 (over z), frame: 2 (over x), row: 4 (over y, core).
Axes of the slice: x: 2, y: 2, z: 4, core: 2. Of those that a mesh axis runs over, the one named last changes fastest.
Arguments:
- clip_input: bfloat16 [4, 8, 16, 240, 128], P('dp', 'frame', 'row'), may hold values from -6 to 6
- cotangent: bfloat16 [4, 8, 16, 240, 128], P('dp', 'frame', 'row'), may hold values from -6 to 6
- spatial_weight: bfloat16 [3, 3, 128, 128], replicated, may hold values from -0.1875 to 0.1875
- temporal_weight: bfloat16 [3, 128, 128], replicated, may hold values from -0.3125 to 0.3125
Outputs:
- block_output: bfloat16 [4, 8, 16, 240, 128], P('dp', 'frame', 'row')
- input_grad: bfloat16 [4, 8, 16, 240, 128], P('dp', 'frame', 'row')
- weight_grads: float32 [1536, 128], P(('dp', 'frame', 'row'))
The draws below stay inside these ranges and needn't reach their ends.
All inputs are finite; a program needn't handle non-finite values.
Results may differ from the reference program's by a relative error of at most 0.0045.
Values may be sent and summed in bfloat16 or wider, within the bound.
A program may use at most 64 MiB of HBM per device.

```python
import math
import jax
import jax.numpy as jnp
from jax import lax

C = 128
W = 240
CLIPS = 4
FRAMES = 8
H = 16
CELLS = 122880


def block_levels(rng, dims, shards, smallest, top_value):
    loudness = 1.0
    for position, shards_of in shards:
        steps = jax.random.uniform(jax.random.fold_in(jax.random.fold_in(rng, 6), position), (shards_of,), jnp.float32, smallest / len(shards), top_value / len(shards))
        loudness = loudness * jnp.repeat(jnp.exp(steps), dims[position] // shards_of).reshape((-1,) + (1,) * (len(dims) - 1 - position))
    return loudness


def noise(key, shape, width, most, pieces=(), held_as=jnp.bfloat16):
    entries = jax.random.normal(key, shape, jnp.float32) * width
    if len(pieces) > 0:
        entries = block_levels(key, shape, pieces, -0.22, 0.18) * entries
    return jnp.clip(entries, min=-most, max=most).astype(held_as)


def setup_inputs(seed: int = 0) -> dict:
    streams_of = jax.random.split(jax.random.key(seed), 5)
    clip_input = noise(streams_of[0], (CLIPS, FRAMES, H, W, C), 1.0, 6.0, ((0, 4), (1, 2), (2, 4)))
    cotangent = noise(streams_of[1], (CLIPS, FRAMES, H, W, C), 1.0, 6.0, ((0, 4), (1, 2), (2, 4)))
    spatial_weight = noise(streams_of[2], (3, 3, C, C), (9 * C) ** -0.5, 0.1875)
    temporal_weight = noise(streams_of[3], (3, C, C), (3 * C) ** -0.5, 0.3125)
    return dict(clip_input=clip_input, cotangent=cotangent, spatial_weight=spatial_weight, temporal_weight=temporal_weight)


def spatial_taps(padded, weights, rows, cols):
    chans = padded.shape[-1]
    total = jnp.zeros((padded.shape[0] * rows * cols, weights.shape[-1]), jnp.float32)
    for i in range(3):
        for j in range(3):
            piece = padded[:, i:i + rows, j:j + cols, :].reshape(-1, chans)
            total = total + jnp.dot(piece, weights[i, j], preferred_element_type=jnp.float32)
    return total.reshape(padded.shape[0], rows, cols, -1)

def contract_rows(left, right):
    return lax.dot_general(left, right, (((0,), (0,)), ((), ())), preferred_element_type=jnp.float32)

def clip_pass(clip_x, clip_g, spatial_weight, temporal_weight):
    frames, rows, cols, chans = clip_x.shape
    xpad = jnp.pad(clip_x, ((0, 0), (1, 1), (1, 1), (0, 0)))
    pre = spatial_taps(xpad, spatial_weight, rows, cols)
    act = jax.nn.silu(pre).astype(jnp.bfloat16)
    act_ext = jnp.pad(act, ((2, 0), (0, 0), (0, 0), (0, 0)))
    grad_ext = jnp.pad(clip_g, ((0, 2), (0, 0), (0, 0), (0, 0)))
    mixed = jnp.zeros((frames * rows * cols, chans), jnp.float32)
    act_grad = jnp.zeros((frames * rows * cols, chans), jnp.float32)
    g_flat = clip_g.reshape(-1, chans)
    temporal_list = []
    for k in range(3):
        shifted = act_ext[2 - k:2 - k + frames].reshape(-1, chans)
        mixed = mixed + jnp.dot(shifted, temporal_weight[k], preferred_element_type=jnp.float32)
        later = grad_ext[k:k + frames].reshape(-1, chans)
        act_grad = act_grad + jnp.dot(later, temporal_weight[k].T, preferred_element_type=jnp.float32)
        temporal_list.append(contract_rows(shifted, g_flat))
    mixed = mixed.astype(jnp.bfloat16).reshape(clip_x.shape)
    block_output = (clip_x.astype(jnp.float32) + mixed.astype(jnp.float32)).astype(jnp.bfloat16)
    act_grad = act_grad.astype(jnp.bfloat16).reshape(clip_x.shape)
    sig = jax.nn.sigmoid(pre)
    pre_grad = (act_grad.astype(jnp.float32) * sig * (1.0 + pre * (1.0 - sig))).astype(jnp.bfloat16)
    pg_flat = pre_grad.reshape(-1, chans)
    spatial_list = []
    for i in range(3):
        for j in range(3):
            piece = xpad[:, i:i + rows, j:j + cols, :].reshape(-1, chans)
            spatial_list.append(contract_rows(piece, pg_flat))
    gpad = jnp.pad(pre_grad, ((0, 0), (1, 1), (1, 1), (0, 0)))
    back = jnp.zeros((frames * rows * cols, chans), jnp.float32)
    for i in range(3):
        for j in range(3):
            piece = gpad[:, 2 - i:2 - i + rows, 2 - j:2 - j + cols, :].reshape(-1, chans)
            back = back + jnp.dot(piece, spatial_weight[i, j].T, preferred_element_type=jnp.float32)
    input_grad = (clip_g.astype(jnp.float32).reshape(-1, chans) + back).astype(jnp.bfloat16).reshape(clip_x.shape)
    grads = jnp.concatenate(spatial_list + temporal_list, axis=0)
    return (block_output, input_grad, grads)

def reference(clip_input, cotangent, spatial_weight, temporal_weight):

    def one_clip(pair):
        return clip_pass(pair[0], pair[1], spatial_weight, temporal_weight)
    outputs, grads_in, grads = lax.map(one_clip, (clip_input, cotangent))
    weight_grads = lax.optimization_barrier(jnp.sum(grads, axis=0)) * (1.0 / math.sqrt(CELLS))
    return (outputs, grads_in, weight_grads)
```

```python
import functools
import math

import jax
import jax.numpy as jnp
from jax import lax
from jax.experimental import pallas as pl
from jax.experimental.pallas import tpu as pltpu
from jax.sharding import PartitionSpec as P

F32 = jnp.float32
BF16 = jnp.bfloat16
MESH = pl.DeviceIdType.MESH


def with_sides(value):
    width = value.shape[0]
    wide = value.astype(F32)
    place = lax.broadcasted_iota(jnp.int32, wide.shape, 0)
    before = jnp.where(place == 0, 0.0, pltpu.roll(wide, 1, 0)).astype(BF16)
    after = jnp.where(place == width - 1, 0.0, pltpu.roll(wide, width - 1, 0)).astype(BF16)
    return jnp.concatenate([before, value, after], axis=1)


def dot(left, right):
    return jnp.dot(left, right, preferred_element_type=F32)


def contract_rows(left, right):
    return lax.dot_general(left, right, (((0,), (0,)), ((), ())), preferred_element_type=F32)


def block_kernel(
    sizes, scale, x_hbm, g_hbm, sw, tw, y_hbm, dx_hbm, wg,
    xv, xh, xc, gv, ax, dv, ag, pc, pe, ph, wf, wb, tf, tb, acc, tacc, part, r1, s1, r2,
    yv, dxv, lsem, osem, xs, xr, cs, cr, as_, ar, ps, pr, s1s, s1r, s2s, s2r,
):
    nd, nf, nr = sizes
    frames, rows, width, chans = x_hbm.shape
    pairs, groups = rows // 2, frames // 2
    scatter = part is not None
    me_d, me_f, me_r = lax.axis_index("dp"), lax.axis_index("frame"), lax.axis_index("row")
    core = me_r % 2
    half = nr // 2
    chips = nd * nf * half
    me_q = (me_d * nf + me_f) * half + me_r // 2
    has_up, has_down = me_r > 0, me_r < nr - 1
    has_prev, has_next = me_f > 0, me_f < nf - 1

    def chip(q):
        return {"dp": q // (nf * half), "frame": (q // half) % nf, "row": 2 * (q % half) + core}

    def remote(src, dst, ssem, rsem, where):
        return pltpu.make_async_remote_copy(
            src_ref=src, dst_ref=dst, send_sem=ssem, recv_sem=rsem,
            device_id=where, device_id_type=MESH,
        )

    load_x = pltpu.make_async_copy(x_hbm, xv, lsem.at[0])
    load_g = pltpu.make_async_copy(g_hbm, gv.at[pl.ds(0, frames)], lsem.at[1])
    load_x.start()

    barrier = pltpu.get_barrier_semaphore()

    def greet(where):
        pl.semaphore_signal(barrier, inc=1, device_id=where, device_id_type=MESH)

    @pl.when(has_up)
    def _():
        greet({"row": me_r - 1})

    @pl.when(has_down)
    def _():
        greet({"row": me_r + 1})

    count = has_up.astype(jnp.int32) + has_down.astype(jnp.int32)
    if scatter:
        def greet_chip(o, carry):
            greet(chip((me_q + o) % chips))
            return carry

        lax.fori_loop(1, chips, greet_chip, 0)
        count = count + (chips - 1)
    else:
        @pl.when(has_prev)
        def _():
            greet({"frame": me_f - 1})

        @pl.when(has_next)
        def _():
            greet({"frame": me_f + 1})

        count = count + has_prev.astype(jnp.int32) + has_next.astype(jnp.int32)
    pl.semaphore_wait(barrier, count)

    x_up = remote(x_hbm.at[:, 0], xh.at[1], xs.at[0], xr.at[1], {"row": me_r - 1})
    x_down = remote(x_hbm.at[:, rows - 1], xh.at[0], xs.at[1], xr.at[0], {"row": me_r + 1})
    g_prev = remote(g_hbm.at[pl.ds(0, 2)], gv.at[pl.ds(frames, 2)], cs, cr, {"frame": me_f - 1})
    a_next = remote(ax.at[pl.ds(frames, 2)], ax.at[pl.ds(0, 2)], as_, ar, {"frame": me_f + 1})
    p_up = remote(pe.at[0], ph.at[1], ps.at[0], pr.at[1], {"row": me_r - 1})
    p_down = remote(pe.at[1], ph.at[0], ps.at[1], pr.at[0], {"row": me_r + 1})
    pl.when(has_up)(x_up.start)
    pl.when(has_down)(x_down.start)
    pl.when(has_prev)(g_prev.start)
    load_g.start()

    zero = jnp.zeros((chans, chans), BF16)
    for a in range(4):
        for b in range(2):
            i = a - b
            cols = pl.ds(b * chans, chans)
            for j in range(3):
                spot = pl.ds((a * 3 + j) * chans, chans)
                wf[spot, cols] = sw[i, j] if 0 <= i <= 2 else zero
                wb[spot, cols] = sw[2 - i, 2 - j].T if 0 <= i <= 2 else zero
            spot = pl.ds(a * chans, chans)
            k = b + 2 - a
            tf[spot, cols] = tw[k] if 0 <= k <= 2 else zero
            tb[spot, cols] = tw[i].T if 0 <= i <= 2 else zero

    load_x.wait()

    def widen(f, carry):
        for r in range(rows):
            xc[f, r + 1] = with_sides(xv[f, r])
        return carry

    lax.fori_loop(0, frames, widen, 0)

    def temporal_in(ref, f):
        return jnp.concatenate(
            [ref[f + a].reshape(rows * width, chans) for a in range(4)], axis=1
        )

    def act_grads(f):
        out = dot(temporal_in(gv, f), tb[...])
        for b in range(2):
            ag[f + b] = out[:, b * chans:(b + 1) * chans].astype(BF16).reshape(rows, width, chans)

    load_g.wait()
    for h in range(groups - 1):
        act_grads(2 * h)

    def halo(has, slot, src, dst, row, copy):
        @pl.when(has)
        def _():
            copy.wait_recv()

            def one(f, carry):
                dst[f, row] = with_sides(src[slot, f])
                return carry

            lax.fori_loop(0, frames, one, 0)

        @pl.when(jnp.logical_not(has))
        def _():
            def one(f, carry):
                dst[f, row] = jnp.zeros((width, 3 * chans), BF16)
                return carry

            lax.fori_loop(0, frames, one, 0)

    halo(has_up, 0, xh, xc, 0, x_down)
    halo(has_down, 1, xh, xc, rows + 1, x_up)

    def conv(src, weight, h, p):
        left = jnp.concatenate(
            [src[2 * h:2 * h + 2, 2 * p + a].reshape(2 * width, 3 * chans) for a in range(4)],
            axis=1,
        )
        return dot(left, weight[...])

    def forward(h):
        for p in range(pairs):
            pre = conv(xc, wf, h, p)
            for b in range(2):
                v = pre[:, b * chans:(b + 1) * chans]
                s = 0.5 + 0.5 * jnp.tanh(0.5 * v)
                shape = (2, width, chans)
                ax[2 * h + 2:2 * h + 4, 2 * p + b] = (v * s).astype(BF16).reshape(shape)
                dv[2 * h:2 * h + 2, 2 * p + b] = (s * (1.0 + v * (1.0 - s))).reshape(shape)

    forward(groups - 1)
    pl.when(has_next)(a_next.start)
    for h in range(groups - 1):
        forward(h)

    def pre_grads(h):
        def one(f, carry):
            for r in range(rows):
                v = (ag[f, r].astype(F32) * dv[f, r]).astype(BF16)
                pc[f, r + 1] = with_sides(v)
                if r == 0:
                    pe[0, f] = v
                if r == rows - 1:
                    pe[1, f] = v
            return carry

        lax.fori_loop(2 * h, 2 * h + 2, one, 0)

    def temporal_term(f):
        left = jnp.concatenate(
            [ax[f + 2 + a].reshape(rows * width, chans) for a in range(2)], axis=1
        )
        return contract_rows(left, temporal_in(gv, f))

    for h in range(groups - 1):
        pre_grads(h)
        if h == 0:
            tacc[...] = temporal_term(0)
        else:
            tacc[...] += temporal_term(2 * h)

    @pl.when(has_next)
    def _():
        g_prev.wait_recv()

    @pl.when(jnp.logical_not(has_next))
    def _():
        gv[frames:frames + 2] = jnp.zeros((2, rows, width, chans), BF16)

    act_grads(frames - 2)
    pre_grads(groups - 1)
    pl.when(has_up)(p_up.start)
    pl.when(has_down)(p_down.start)
    if groups > 1:
        tacc[...] += temporal_term(frames - 2)
    else:
        tacc[...] = temporal_term(frames - 2)

    for p in range(pairs):
        right = jnp.concatenate(
            [
                pc[:, 2 * p + 1 + b, :, chans:2 * chans].reshape(frames * width, chans)
                for b in range(2)
            ],
            axis=1,
        )
        for a in range(4):
            term = contract_rows(xc[:, 2 * p + a].reshape(frames * width, 3 * chans), right)
            if p == 0:
                acc[a] = term
            else:
                acc[a] += term

    def put(tap, value):
        if not scatter:
            wg[tap * chans:(tap + 1) * chans] = value
            return
        blocks = part.shape[2]
        for n in range(chans // 16):
            at = tap * (chans // 16) + n
            owner = at // blocks
            part[owner // 2, owner % 2, at % blocks] = value[n * 16:(n + 1) * 16]

    for i in range(3):
        for j in range(3):
            spot = pl.ds(j * chans, chans)
            put(i * 3 + j, acc[i, spot, 0:chans] + acc[i + 1, spot, chans:2 * chans])
    for k in range(3):
        total = None
        for a in range(2):
            piece = tacc[a * chans:(a + 1) * chans, (a + k) * chans:(a + k + 1) * chans]
            total = piece if total is None else total + piece
        put(9 + k, total)

    if scatter:
        core_copy = remote(part.at[:, 1 - core], r1, s1s, s1r, {"row": me_r + 1 - 2 * core})
        core_copy.start()

    def mix(h):
        out = dot(temporal_in(ax, 2 * h), tf[...])
        for b in range(2):
            f = 2 * h + b
            mixed = out[:, b * chans:(b + 1) * chans].astype(BF16).astype(F32)
            x = xc[f, 1:rows + 1, :, chans:2 * chans].reshape(rows * width, chans).astype(F32)
            yv[f] = (x + mixed).astype(BF16).reshape(rows, width, chans)
        spot = pl.ds(2 * h, 2)
        copy = pltpu.make_async_copy(yv.at[spot], y_hbm.at[spot], osem.at[h])
        copy.start()
        return copy

    outs = [mix(h) for h in range(1, groups)]

    if scatter:
        core_copy.wait_recv()

        def narrow(q, carry):
            s1[q] = (part[q, core] + r1[q]).astype(BF16)
            return carry

        lax.fori_loop(0, chips, narrow, 0)

        def to_chip(o):
            q = (me_q + o) % chips
            return remote(s1.at[q], r2.at[me_q], s2s.at[o], s2r.at[me_q], chip(q))

        def send(o, carry):
            to_chip(o).start()
            return carry

        lax.fori_loop(1, chips, send, 0)

    halo(has_up, 0, ph, pc, 0, p_down)
    halo(has_down, 1, ph, pc, rows + 1, p_up)
    for h in range(groups):
        for p in range(pairs):
            back = conv(pc, wb, h, p)
            for b in range(2):
                g = gv[2 * h:2 * h + 2, 2 * p + b].reshape(2 * width, chans).astype(F32)
                v = (g + back[:, b * chans:(b + 1) * chans]).astype(BF16)
                dxv[2 * h:2 * h + 2, 2 * p + b] = v.reshape(2, width, chans)
        spot = pl.ds(2 * h, 2)
        copy = pltpu.make_async_copy(dxv.at[spot], dx_hbm.at[spot], osem.at[groups + h])
        copy.start()
        outs.append(copy)

    @pl.when(has_prev)
    def _():
        a_next.wait_recv()

    @pl.when(jnp.logical_not(has_prev))
    def _():
        ax[0:2] = jnp.zeros((2, rows, width, chans), BF16)

    outs.append(mix(0))

    if scatter:
        wg[...] = (part[me_q, core] + r1[me_q]).reshape(wg.shape)

        def collect(o, carry):
            q = (me_q + chips - o) % chips
            remote(s1.at[q], r2.at[q], s2s.at[o], s2r.at[q], chip(q)).wait_recv()
            wg[...] += r2[q].astype(F32).reshape(wg.shape)
            to_chip(o).wait_send()
            return carry

        lax.fori_loop(1, chips, collect, 0)
        wg[...] = wg[...] * scale
        core_copy.wait_send()

    pl.when(has_up)(x_up.wait_send)
    pl.when(has_down)(x_down.wait_send)
    pl.when(has_prev)(g_prev.wait_send)
    pl.when(has_next)(a_next.wait_send)
    pl.when(has_up)(p_up.wait_send)
    pl.when(has_down)(p_down.wait_send)
    for copy in outs:
        copy.wait()


def on_device(sizes, clip_input, cotangent, spatial_weight, temporal_weight):
    x, g = clip_input[0], cotangent[0]
    frames, rows, width, chans = x.shape
    nd, nf, nr = sizes
    devices = nd * nf * nr
    scale = 1.0 / math.sqrt(nd * frames * nf * rows * nr * width)
    terms = 12 * chans
    own = terms // devices
    scatter = own % 16 == 0 and terms % devices == 0 and nr % 2 == 0
    chips = devices // 2
    blocks = own // 16
    dma, regular = pltpu.SemaphoreType.DMA, pltpu.VMEM
    scratch = [
        regular((frames, rows, width, chans), BF16),
        regular((2, frames, width, chans), BF16),
        regular((frames, rows + 2, width, 3 * chans), BF16),
        regular((frames + 2, rows, width, chans), BF16),
        regular((frames + 2, rows, width, chans), BF16),
        regular((frames, rows, width, chans), F32),
        regular((frames, rows, width, chans), BF16),
        regular((frames, rows + 2, width, 3 * chans), BF16),
        regular((2, frames, width, chans), BF16),
        regular((2, frames, width, chans), BF16),
        regular((12 * chans, 2 * chans), BF16),
        regular((12 * chans, 2 * chans), BF16),
        regular((4 * chans, 2 * chans), BF16),
        regular((4 * chans, 2 * chans), BF16),
        regular((4, 3 * chans, 2 * chans), F32),
        regular((2 * chans, 4 * chans), F32),
    ]
    if scatter:
        scratch += [
            regular((chips, 2, blocks, 16, chans), F32),
            regular((chips, blocks, 16, chans), F32),
            regular((chips, blocks, 16, chans), BF16),
            regular((chips, blocks, 16, chans), BF16),
        ]
    scratch += [
        regular((frames, rows, width, chans), BF16),
        regular((frames, rows, width, chans), BF16),
        dma((2,)), dma((frames,)),
        dma((2,)), dma((2,)), dma, dma, dma, dma, dma((2,)), dma((2,)),
    ]
    if scatter:
        scratch += [dma, dma, dma((chips,)), dma((chips,))]

    def kernel(*refs):
        refs = list(refs)
        if not scatter:
            refs[23:23] = [None] * 4
            refs += [None] * 4
        block_kernel(sizes, scale, *refs)

    whole = jax.ShapeDtypeStruct(x.shape, BF16)
    grads = jax.ShapeDtypeStruct((own if scatter else terms, chans), F32)
    anywhere = pl.BlockSpec(memory_space=pl.ANY)
    vmem = pl.BlockSpec(memory_space=pltpu.VMEM)
    y, dx, wg = pl.pallas_call(
        kernel,
        out_shape=(whole, whole, grads),
        in_specs=[anywhere, anywhere, vmem, vmem],
        out_specs=(anywhere, anywhere, vmem),
        scratch_shapes=scratch,
        compiler_params=pltpu.CompilerParams(
            collective_id=0, has_side_effects=True, vmem_limit_bytes=56 * 1024 * 1024
        ),
    )(x, g, spatial_weight, temporal_weight)
    if not scatter:
        wg = scale * lax.psum_scatter(
            wg, ("dp", "frame", "row"), scatter_dimension=0, tiled=True
        )
    return (y[None], dx[None], wg)


def solution(mesh):
    spread = P("dp", "frame", "row", None, None)
    sizes = tuple(mesh.shape[name] for name in ("dp", "frame", "row"))
    return jax.shard_map(
        functools.partial(on_device, sizes),
        mesh=mesh,
        in_specs=(spread, spread, P(), P()),
        out_specs=(spread, spread, P(("dp", "frame", "row"), None)),
        check_vma=False,
    )
```

```python
import functools
import math

import jax
import jax.numpy as jnp
from jax import lax
from jax.experimental import pallas as pl
from jax.experimental.pallas import tpu as pltpu
from jax.sharding import PartitionSpec as P

F32 = jnp.float32
BF16 = jnp.bfloat16
MESH = pl.DeviceIdType.MESH


def with_sides(value):
    width = value.shape[0]
    wide = value.astype(F32)
    place = lax.broadcasted_iota(jnp.int32, wide.shape, 0)
    before = jnp.where(place == 0, 0.0, pltpu.roll(wide, 1, 0)).astype(BF16)
    after = jnp.where(place == width - 1, 0.0, pltpu.roll(wide, width - 1, 0)).astype(BF16)
    return jnp.concatenate([before, value, after], axis=1)


def dot(left, right):
    return jnp.dot(left, right, preferred_element_type=F32)


def contract_rows(left, right):
    return lax.dot_general(left, right, (((0,), (0,)), ((), ())), preferred_element_type=F32)


def block_kernel(
    sizes, scale, x_hbm, g_hbm, sw, tw, y_hbm, dx_hbm, wg,
    xv, xh, xc, gv, ax, dv, ag, pc, pe, ph, wf, wb, tf, tb, acc, tacc, part, r1, s1, r2,
    yv, dxv, lsem, osem, xs, xr, cs, cr, as_, ar, ps, pr, s1s, s1r, s2s, s2r,
):
    nd, nf, nr = sizes
    frames, rows, width, chans = x_hbm.shape
    pairs, groups = rows // 2, frames // 2
    scatter = part is not None
    me_d, me_f, me_r = lax.axis_index("dp"), lax.axis_index("frame"), lax.axis_index("row")
    core = me_r % 2
    half = nr // 2
    chips = nd * nf * half
    me_q = (me_d * nf + me_f) * half + me_r // 2
    has_up, has_down = me_r > 0, me_r < nr - 1
    has_prev, has_next = me_f > 0, me_f < nf - 1

    def chip(q):
        return {"dp": q // (nf * half), "frame": (q // half) % nf, "row": 2 * (q % half) + core}

    def remote(src, dst, ssem, rsem, where):
        return pltpu.make_async_remote_copy(
            src_ref=src, dst_ref=dst, send_sem=ssem, recv_sem=rsem,
            device_id=where, device_id_type=MESH,
        )

    load_x = pltpu.make_async_copy(x_hbm, xv, lsem.at[0])
    load_g = pltpu.make_async_copy(g_hbm, gv.at[pl.ds(0, frames)], lsem.at[1])
    load_x.start()

    barrier = pltpu.get_barrier_semaphore()

    def greet(where):
        pl.semaphore_signal(barrier, inc=1, device_id=where, device_id_type=MESH)

    @pl.when(has_up)
    def _():
        greet({"row": me_r - 1})

    @pl.when(has_down)
    def _():
        greet({"row": me_r + 1})

    count = has_up.astype(jnp.int32) + has_down.astype(jnp.int32)
    if scatter:
        def greet_chip(o, carry):
            greet(chip((me_q + o) % chips))
            return carry

        lax.fori_loop(1, chips, greet_chip, 0)
        count = count + (chips - 1)
    else:
        @pl.when(has_prev)
        def _():
            greet({"frame": me_f - 1})

        @pl.when(has_next)
        def _():
            greet({"frame": me_f + 1})

        count = count + has_prev.astype(jnp.int32) + has_next.astype(jnp.int32)
    pl.semaphore_wait(barrier, count)

    x_up = remote(x_hbm.at[:, 0], xh.at[1], xs.at[0], xr.at[1], {"row": me_r - 1})
    x_down = remote(x_hbm.at[:, rows - 1], xh.at[0], xs.at[1], xr.at[0], {"row": me_r + 1})
    g_prev = [
        remote(
            g_hbm.at[pl.ds(0, 2), pl.ds(2 * p, 2)], gv.at[pl.ds(frames, 2), pl.ds(2 * p, 2)],
            cs.at[p], cr.at[p], {"frame": me_f - 1},
        )
        for p in range(pairs)
    ]
    a_next = remote(ax.at[pl.ds(frames, 2)], ax.at[pl.ds(0, 2)], as_, ar, {"frame": me_f + 1})
    p_up, p_down = [], []
    for h in range(groups):
        spot = pl.ds(2 * h, 2)
        p_up.append(remote(
            pe.at[0, spot], ph.at[1, spot], ps.at[0, h], pr.at[1, h], {"row": me_r - 1}
        ))
        p_down.append(remote(
            pe.at[1, spot], ph.at[0, spot], ps.at[1, h], pr.at[0, h], {"row": me_r + 1}
        ))
    pl.when(has_up)(x_up.start)
    pl.when(has_down)(x_down.start)
    for copy in g_prev:
        pl.when(has_prev)(copy.start)
    load_g.start()

    zero = jnp.zeros((chans, chans), BF16)
    for a in range(4):
        for b in range(2):
            i = a - b
            cols = pl.ds(b * chans, chans)
            for j in range(3):
                spot = pl.ds((a * 3 + j) * chans, chans)
                wf[spot, cols] = sw[i, j] if 0 <= i <= 2 else zero
                wb[spot, cols] = sw[2 - i, 2 - j].T if 0 <= i <= 2 else zero
            spot = pl.ds(a * chans, chans)
            k = b + 2 - a
            tf[spot, cols] = tw[k] if 0 <= k <= 2 else zero
            tb[spot, cols] = tw[i].T if 0 <= i <= 2 else zero

    load_x.wait()

    def widen(f, carry):
        for r in range(rows):
            xc[f, r + 1] = with_sides(xv[f, r])
        return carry

    lax.fori_loop(0, frames, widen, 0)

    def temporal_in(ref, f, lo, hi):
        return jnp.concatenate(
            [ref[f + a, lo:hi].reshape((hi - lo) * width, chans) for a in range(4)], axis=1
        )

    def act_grads(f, lo, hi):
        out = dot(temporal_in(gv, f, lo, hi), tb[...])
        for b in range(2):
            v = out[:, b * chans:(b + 1) * chans].astype(BF16)
            ag[f + b, lo:hi] = v.reshape(hi - lo, width, chans)

    load_g.wait()
    for h in range(groups - 1):
        act_grads(2 * h, 0, rows)

    def halo(has, slot, src, dst, row, copy, first, last):
        @pl.when(has)
        def _():
            copy.wait_recv()

            def one(f, carry):
                dst[f, row] = with_sides(src[slot, f])
                return carry

            lax.fori_loop(first, last, one, 0)

        @pl.when(jnp.logical_not(has))
        def _():
            def one(f, carry):
                dst[f, row] = jnp.zeros((width, 3 * chans), BF16)
                return carry

            lax.fori_loop(first, last, one, 0)

    halo(has_up, 0, xh, xc, 0, x_down, 0, frames)
    halo(has_down, 1, xh, xc, rows + 1, x_up, 0, frames)

    def conv(src, weight, h, p):
        left = jnp.concatenate(
            [src[2 * h:2 * h + 2, 2 * p + a].reshape(2 * width, 3 * chans) for a in range(4)],
            axis=1,
        )
        return dot(left, weight[...])

    def forward(h):
        for p in range(pairs):
            pre = conv(xc, wf, h, p)
            for b in range(2):
                v = pre[:, b * chans:(b + 1) * chans]
                s = 0.5 + 0.5 * jnp.tanh(0.5 * v)
                shape = (2, width, chans)
                ax[2 * h + 2:2 * h + 4, 2 * p + b] = (v * s).astype(BF16).reshape(shape)
                dv[2 * h:2 * h + 2, 2 * p + b] = (s * (1.0 + v * (1.0 - s))).reshape(shape)

    forward(groups - 1)
    pl.when(has_next)(a_next.start)
    for h in range(groups - 1):
        forward(h)

    def pre_grads(h, lo, hi):
        def one(f, carry):
            for r in range(lo, hi):
                v = (ag[f, r].astype(F32) * dv[f, r]).astype(BF16)
                pc[f, r + 1] = with_sides(v)
                if r == 0:
                    pe[0, f] = v
                if r == rows - 1:
                    pe[1, f] = v
            return carry

        lax.fori_loop(2 * h, 2 * h + 2, one, 0)

    def temporal_term(h, lo, hi, fresh):
        f = 2 * h
        left = jnp.concatenate(
            [ax[f + 2 + a, lo:hi].reshape((hi - lo) * width, chans) for a in range(2)], axis=1
        )
        term = contract_rows(left, temporal_in(gv, f, lo, hi))
        if fresh:
            tacc[...] = term
        else:
            tacc[...] += term

    def spatial_term(h, p, fresh):
        right = jnp.concatenate(
            [
                pc[2 * h:2 * h + 2, 2 * p + 1 + b, :, chans:2 * chans].reshape(2 * width, chans)
                for b in range(2)
            ],
            axis=1,
        )
        for a in range(4):
            left = xc[2 * h:2 * h + 2, 2 * p + a].reshape(2 * width, 3 * chans)
            term = contract_rows(left, right)
            if fresh:
                acc[a] = term
            else:
                acc[a] += term

    def send_edges(h):
        pl.when(has_up)(p_up[h].start)
        pl.when(has_down)(p_down[h].start)

    def mix(h):
        out = dot(temporal_in(ax, 2 * h, 0, rows), tf[...])
        for b in range(2):
            f = 2 * h + b
            mixed = out[:, b * chans:(b + 1) * chans].astype(BF16).astype(F32)
            x = xc[f, 1:rows + 1, :, chans:2 * chans].reshape(rows * width, chans).astype(F32)
            yv[f] = (x + mixed).astype(BF16).reshape(rows, width, chans)
        spot = pl.ds(2 * h, 2)
        copy = pltpu.make_async_copy(yv.at[spot], y_hbm.at[spot], osem.at[h])
        copy.start()
        return copy

    def backward(h):
        halo(has_up, 0, ph, pc, 0, p_down[h], 2 * h, 2 * h + 2)
        halo(has_down, 1, ph, pc, rows + 1, p_up[h], 2 * h, 2 * h + 2)
        for p in range(pairs):
            back = conv(pc, wb, h, p)
            for b in range(2):
                g = gv[2 * h:2 * h + 2, 2 * p + b].reshape(2 * width, chans).astype(F32)
                v = (g + back[:, b * chans:(b + 1) * chans]).astype(BF16)
                dxv[2 * h:2 * h + 2, 2 * p + b] = v.reshape(2, width, chans)
        spot = pl.ds(2 * h, 2)
        copy = pltpu.make_async_copy(dxv.at[spot], dx_hbm.at[spot], osem.at[groups + h])
        copy.start()
        return copy

    outs = []
    for h in range(groups - 1):
        pre_grads(h, 0, rows)
        send_edges(h)
        temporal_term(h, 0, rows, h == 0)
        for p in range(pairs):
            spatial_term(h, p, h == 0 and p == 0)
    for h in range(1, groups):
        outs.append(mix(h))
    for h in range(groups - 1):
        outs.append(backward(h))

    for p in range(pairs):
        lo, hi = 2 * p, 2 * p + 2

        @pl.when(has_next)
        def _():
            g_prev[p].wait_recv()

        @pl.when(jnp.logical_not(has_next))
        def _():
            gv[frames:frames + 2, lo:hi] = jnp.zeros((2, 2, width, chans), BF16)

        act_grads(frames - 2, lo, hi)
        pre_grads(groups - 1, lo, hi)
        if p == pairs - 1:
            send_edges(groups - 1)
        temporal_term(groups - 1, lo, hi, groups == 1 and p == 0)
        spatial_term(groups - 1, p, groups == 1 and p == 0)

    def put(tap, value):
        if not scatter:
            wg[tap * chans:(tap + 1) * chans] = value
            return
        blocks = part.shape[2]
        for n in range(chans // 16):
            at = tap * (chans // 16) + n
            owner = at // blocks
            part[owner // 2, owner % 2, at % blocks] = value[n * 16:(n + 1) * 16]

    for i in range(3):
        for j in range(3):
            spot = pl.ds(j * chans, chans)
            put(i * 3 + j, acc[i, spot, 0:chans] + acc[i + 1, spot, chans:2 * chans])
    for k in range(3):
        total = None
        for a in range(2):
            piece = tacc[a * chans:(a + 1) * chans, (a + k) * chans:(a + k + 1) * chans]
            total = piece if total is None else total + piece
        put(9 + k, total)

    if scatter:
        core_copy = remote(part.at[:, 1 - core], r1, s1s, s1r, {"row": me_r + 1 - 2 * core})
        core_copy.start()

    if scatter:
        core_copy.wait_recv()

        def narrow(q, carry):
            s1[q] = (part[q, core] + r1[q]).astype(BF16)
            return carry

        lax.fori_loop(0, chips, narrow, 0)

        def to_chip(o):
            q = (me_q + o) % chips
            return remote(s1.at[q], r2.at[me_q], s2s.at[o], s2r.at[me_q], chip(q))

        def send(o, carry):
            to_chip(o).start()
            return carry

        lax.fori_loop(1, chips, send, 0)

    outs.append(backward(groups - 1))

    @pl.when(has_prev)
    def _():
        a_next.wait_recv()

    @pl.when(jnp.logical_not(has_prev))
    def _():
        ax[0:2] = jnp.zeros((2, rows, width, chans), BF16)

    outs.append(mix(0))

    if scatter:
        wg[...] = (part[me_q, core] + r1[me_q]).reshape(wg.shape)

        def collect(o, carry):
            q = (me_q + chips - o) % chips
            remote(s1.at[q], r2.at[q], s2s.at[o], s2r.at[q], chip(q)).wait_recv()
            wg[...] += r2[q].astype(F32).reshape(wg.shape)
            to_chip(o).wait_send()
            return carry

        lax.fori_loop(1, chips, collect, 0)
        wg[...] = wg[...] * scale
        core_copy.wait_send()

    pl.when(has_up)(x_up.wait_send)
    pl.when(has_down)(x_down.wait_send)
    for copy in g_prev:
        pl.when(has_prev)(copy.wait_send)
    pl.when(has_next)(a_next.wait_send)
    for h in range(groups):
        pl.when(has_up)(p_up[h].wait_send)
        pl.when(has_down)(p_down[h].wait_send)
    for copy in outs:
        copy.wait()


def on_device(sizes, clip_input, cotangent, spatial_weight, temporal_weight):
    x, g = clip_input[0], cotangent[0]
    frames, rows, width, chans = x.shape
    nd, nf, nr = sizes
    devices = nd * nf * nr
    scale = 1.0 / math.sqrt(nd * frames * nf * rows * nr * width)
    terms = 12 * chans
    own = terms // devices
    scatter = own % 16 == 0 and terms % devices == 0 and nr % 2 == 0
    chips = devices // 2
    blocks = own // 16
    dma, regular = pltpu.SemaphoreType.DMA, pltpu.VMEM
    scratch = [
        regular((frames, rows, width, chans), BF16),
        regular((2, frames, width, chans), BF16),
        regular((frames, rows + 2, width, 3 * chans), BF16),
        regular((frames + 2, rows, width, chans), BF16),
        regular((frames + 2, rows, width, chans), BF16),
        regular((frames, rows, width, chans), F32),
        regular((frames, rows, width, chans), BF16),
        regular((frames, rows + 2, width, 3 * chans), BF16),
        regular((2, frames, width, chans), BF16),
        regular((2, frames, width, chans), BF16),
        regular((12 * chans, 2 * chans), BF16),
        regular((12 * chans, 2 * chans), BF16),
        regular((4 * chans, 2 * chans), BF16),
        regular((4 * chans, 2 * chans), BF16),
        regular((4, 3 * chans, 2 * chans), F32),
        regular((2 * chans, 4 * chans), F32),
    ]
    if scatter:
        scratch += [
            regular((chips, 2, blocks, 16, chans), F32),
            regular((chips, blocks, 16, chans), F32),
            regular((chips, blocks, 16, chans), BF16),
            regular((chips, blocks, 16, chans), BF16),
        ]
    scratch += [
        regular((frames, rows, width, chans), BF16),
        regular((frames, rows, width, chans), BF16),
        dma((2,)), dma((frames,)),
        dma((2,)), dma((2,)), dma((rows // 2,)), dma((rows // 2,)), dma, dma,
        dma((2, frames // 2)), dma((2, frames // 2)),
    ]
    if scatter:
        scratch += [dma, dma, dma((chips,)), dma((chips,))]

    def kernel(*refs):
        refs = list(refs)
        if not scatter:
            refs[23:23] = [None] * 4
            refs += [None] * 4
        block_kernel(sizes, scale, *refs)

    whole = jax.ShapeDtypeStruct(x.shape, BF16)
    grads = jax.ShapeDtypeStruct((own if scatter else terms, chans), F32)
    anywhere = pl.BlockSpec(memory_space=pl.ANY)
    vmem = pl.BlockSpec(memory_space=pltpu.VMEM)
    y, dx, wg = pl.pallas_call(
        kernel,
        out_shape=(whole, whole, grads),
        in_specs=[anywhere, anywhere, vmem, vmem],
        out_specs=(anywhere, anywhere, vmem),
        scratch_shapes=scratch,
        compiler_params=pltpu.CompilerParams(
            collective_id=0, has_side_effects=True, vmem_limit_bytes=56 * 1024 * 1024
        ),
    )(x, g, spatial_weight, temporal_weight)
    if not scatter:
        wg = scale * lax.psum_scatter(
            wg, ("dp", "frame", "row"), scatter_dimension=0, tiled=True
        )
    return (y[None], dx[None], wg)


def solution(mesh):
    spread = P("dp", "frame", "row", None, None)
    sizes = tuple(mesh.shape[name] for name in ("dp", "frame", "row"))
    return jax.shard_map(
        functools.partial(on_device, sizes),
        mesh=mesh,
        in_specs=(spread, spread, P(), P()),
        out_specs=(spread, spread, P(("dp", "frame", "row"), None)),
        check_vma=False,
    )
```

```python
import functools
import math

import jax
import jax.numpy as jnp
from jax import lax
from jax.experimental import pallas as pl
from jax.experimental.pallas import tpu as pltpu
from jax.sharding import PartitionSpec as P

F32 = jnp.float32
BF16 = jnp.bfloat16
MESH = pl.DeviceIdType.MESH


def with_sides(value):
    width = value.shape[0]
    wide = value.astype(F32)
    place = lax.broadcasted_iota(jnp.int32, wide.shape, 0)
    before = jnp.where(place == 0, 0.0, pltpu.roll(wide, 1, 0)).astype(BF16)
    after = jnp.where(place == width - 1, 0.0, pltpu.roll(wide, width - 1, 0)).astype(BF16)
    return jnp.concatenate([before, value, after], axis=1)


def dot(left, right):
    return jnp.dot(left, right, preferred_element_type=F32)


def contract_rows(left, right):
    return lax.dot_general(left, right, (((0,), (0,)), ((), ())), preferred_element_type=F32)


def block_kernel(
    sizes, scale, x_hbm, g_hbm, sw, tw, y_hbm, dx_hbm, wg,
    xv, xh, xc, gv, ax, dv, ag, pc, pe, ph, wf, wb, tf, tb, acc, tacc, part, r1, s1, r2,
    s3, r3, yv, dxv, lsem, osem, xs, xr, cs, cr, as_, ar, ps, pr, s1s, s1r, s2s, s2r, s3s, s3r,
):
    nd, nf, nr = sizes
    frames, rows, width, chans = x_hbm.shape
    pairs, groups = rows // 2, frames // 2
    scatter = part is not None
    me_d, me_f, me_r = lax.axis_index("dp"), lax.axis_index("frame"), lax.axis_index("row")
    core = me_r % 2
    half = nr // 2
    chips = nd * nf * half
    plane = nf * half
    me_p = me_f * half + me_r // 2
    me_q = me_d * plane + me_p
    has_up, has_down = me_r > 0, me_r < nr - 1
    has_prev, has_next = me_f > 0, me_f < nf - 1

    def chip(p):
        return {"frame": p // half, "row": 2 * (p % half) + core}

    def remote(src, dst, ssem, rsem, where):
        return pltpu.make_async_remote_copy(
            src_ref=src, dst_ref=dst, send_sem=ssem, recv_sem=rsem,
            device_id=where, device_id_type=MESH,
        )

    load_x = pltpu.make_async_copy(x_hbm, xv, lsem.at[0])
    load_g = pltpu.make_async_copy(g_hbm, gv.at[pl.ds(0, frames)], lsem.at[1])
    load_x.start()

    barrier = pltpu.get_barrier_semaphore()

    def greet(where):
        pl.semaphore_signal(barrier, inc=1, device_id=where, device_id_type=MESH)

    @pl.when(has_up)
    def _():
        greet({"row": me_r - 1})

    @pl.when(has_down)
    def _():
        greet({"row": me_r + 1})

    count = has_up.astype(jnp.int32) + has_down.astype(jnp.int32)
    if scatter:
        def greet_chip(o, carry):
            greet(chip((me_p + o) % plane))
            return carry

        lax.fori_loop(1, plane, greet_chip, 0)
        for o in range(1, nd):
            greet({"dp": (me_d + o) % nd})
        count = count + (plane - 1) + (nd - 1)
    else:
        @pl.when(has_prev)
        def _():
            greet({"frame": me_f - 1})

        @pl.when(has_next)
        def _():
            greet({"frame": me_f + 1})

        count = count + has_prev.astype(jnp.int32) + has_next.astype(jnp.int32)
    pl.semaphore_wait(barrier, count)

    x_up = remote(x_hbm.at[:, 0], xh.at[1], xs.at[0], xr.at[1], {"row": me_r - 1})
    x_down = remote(x_hbm.at[:, rows - 1], xh.at[0], xs.at[1], xr.at[0], {"row": me_r + 1})
    g_prev = [
        remote(
            g_hbm.at[pl.ds(0, 2), pl.ds(2 * p, 2)], gv.at[pl.ds(frames, 2), pl.ds(2 * p, 2)],
            cs.at[p], cr.at[p], {"frame": me_f - 1},
        )
        for p in range(pairs)
    ]
    a_next = remote(ax.at[pl.ds(frames, 2)], ax.at[pl.ds(0, 2)], as_, ar, {"frame": me_f + 1})
    p_up, p_down = [], []
    for h in range(groups):
        spot = pl.ds(2 * h, 2)
        p_up.append(remote(
            pe.at[0, spot], ph.at[1, spot], ps.at[0, h], pr.at[1, h], {"row": me_r - 1}
        ))
        p_down.append(remote(
            pe.at[1, spot], ph.at[0, spot], ps.at[1, h], pr.at[0, h], {"row": me_r + 1}
        ))
    pl.when(has_up)(x_up.start)
    pl.when(has_down)(x_down.start)
    for copy in g_prev:
        pl.when(has_prev)(copy.start)
    load_g.start()

    zero = jnp.zeros((chans, chans), BF16)
    for a in range(4):
        for b in range(2):
            i = a - b
            cols = pl.ds(b * chans, chans)
            for j in range(3):
                spot = pl.ds((a * 3 + j) * chans, chans)
                wf[spot, cols] = sw[i, j] if 0 <= i <= 2 else zero
                wb[spot, cols] = sw[2 - i, 2 - j].T if 0 <= i <= 2 else zero
            spot = pl.ds(a * chans, chans)
            k = b + 2 - a
            tf[spot, cols] = tw[k] if 0 <= k <= 2 else zero
            tb[spot, cols] = tw[i].T if 0 <= i <= 2 else zero

    load_x.wait()

    def widen(f, carry):
        for r in range(rows):
            xc[f, r + 1] = with_sides(xv[f, r])
        return carry

    lax.fori_loop(0, frames, widen, 0)

    def temporal_in(ref, f, lo, hi):
        return jnp.concatenate(
            [ref[f + a, lo:hi].reshape((hi - lo) * width, chans) for a in range(4)], axis=1
        )

    def act_grads(f, lo, hi):
        out = dot(temporal_in(gv, f, lo, hi), tb[...])
        for b in range(2):
            v = out[:, b * chans:(b + 1) * chans].astype(BF16)
            ag[f + b, lo:hi] = v.reshape(hi - lo, width, chans)

    load_g.wait()
    for h in range(groups - 1):
        act_grads(2 * h, 0, rows)

    def halo(has, slot, src, dst, row, copy, first, last):
        @pl.when(has)
        def _():
            copy.wait_recv()

            def one(f, carry):
                dst[f, row] = with_sides(src[slot, f])
                return carry

            lax.fori_loop(first, last, one, 0)

        @pl.when(jnp.logical_not(has))
        def _():
            def one(f, carry):
                dst[f, row] = jnp.zeros((width, 3 * chans), BF16)
                return carry

            lax.fori_loop(first, last, one, 0)

    halo(has_up, 0, xh, xc, 0, x_down, 0, frames)
    halo(has_down, 1, xh, xc, rows + 1, x_up, 0, frames)

    def conv(src, weight, h, p):
        left = jnp.concatenate(
            [src[2 * h:2 * h + 2, 2 * p + a].reshape(2 * width, 3 * chans) for a in range(4)],
            axis=1,
        )
        return dot(left, weight[...])

    def forward(h):
        for p in range(pairs):
            pre = conv(xc, wf, h, p)
            for b in range(2):
                v = pre[:, b * chans:(b + 1) * chans]
                s = 0.5 + 0.5 * jnp.tanh(0.5 * v)
                shape = (2, width, chans)
                ax[2 * h + 2:2 * h + 4, 2 * p + b] = (v * s).astype(BF16).reshape(shape)
                dv[2 * h:2 * h + 2, 2 * p + b] = (s * (1.0 + v * (1.0 - s))).reshape(shape)

    forward(groups - 1)
    pl.when(has_next)(a_next.start)
    for h in range(groups - 1):
        forward(h)

    def pre_grads(h, lo, hi):
        def one(f, carry):
            for r in range(lo, hi):
                v = (ag[f, r].astype(F32) * dv[f, r]).astype(BF16)
                pc[f, r + 1] = with_sides(v)
                if r == 0:
                    pe[0, f] = v
                if r == rows - 1:
                    pe[1, f] = v
            return carry

        lax.fori_loop(2 * h, 2 * h + 2, one, 0)

    def temporal_term(h, lo, hi, fresh):
        f = 2 * h
        left = jnp.concatenate(
            [ax[f + 2 + a, lo:hi].reshape((hi - lo) * width, chans) for a in range(2)], axis=1
        )
        term = contract_rows(left, temporal_in(gv, f, lo, hi))
        if fresh:
            tacc[...] = term
        else:
            tacc[...] += term

    def spatial_term(h, p, fresh):
        right = jnp.concatenate(
            [
                pc[2 * h:2 * h + 2, 2 * p + 1 + b, :, chans:2 * chans].reshape(2 * width, chans)
                for b in range(2)
            ],
            axis=1,
        )
        for a in range(4):
            left = xc[2 * h:2 * h + 2, 2 * p + a].reshape(2 * width, 3 * chans)
            term = contract_rows(left, right)
            if fresh:
                acc[a] = term
            else:
                acc[a] += term

    def send_edges(h):
        pl.when(has_up)(p_up[h].start)
        pl.when(has_down)(p_down[h].start)

    def mix(h):
        out = dot(temporal_in(ax, 2 * h, 0, rows), tf[...])
        for b in range(2):
            f = 2 * h + b
            mixed = out[:, b * chans:(b + 1) * chans].astype(BF16).astype(F32)
            x = xc[f, 1:rows + 1, :, chans:2 * chans].reshape(rows * width, chans).astype(F32)
            yv[f] = (x + mixed).astype(BF16).reshape(rows, width, chans)
        spot = pl.ds(2 * h, 2)
        copy = pltpu.make_async_copy(yv.at[spot], y_hbm.at[spot], osem.at[h])
        copy.start()
        return copy

    def backward(h):
        halo(has_up, 0, ph, pc, 0, p_down[h], 2 * h, 2 * h + 2)
        halo(has_down, 1, ph, pc, rows + 1, p_up[h], 2 * h, 2 * h + 2)
        for p in range(pairs):
            back = conv(pc, wb, h, p)
            for b in range(2):
                g = gv[2 * h:2 * h + 2, 2 * p + b].reshape(2 * width, chans).astype(F32)
                v = (g + back[:, b * chans:(b + 1) * chans]).astype(BF16)
                dxv[2 * h:2 * h + 2, 2 * p + b] = v.reshape(2, width, chans)
        spot = pl.ds(2 * h, 2)
        copy = pltpu.make_async_copy(dxv.at[spot], dx_hbm.at[spot], osem.at[groups + h])
        copy.start()
        return copy

    outs = []
    for h in range(groups - 1):
        pre_grads(h, 0, rows)
        send_edges(h)
        temporal_term(h, 0, rows, h == 0)
        for p in range(pairs):
            spatial_term(h, p, h == 0 and p == 0)
    for h in range(1, groups):
        outs.append(mix(h))
    for h in range(groups - 1):
        outs.append(backward(h))

    for p in range(pairs):
        lo, hi = 2 * p, 2 * p + 2

        @pl.when(has_next)
        def _():
            g_prev[p].wait_recv()

        @pl.when(jnp.logical_not(has_next))
        def _():
            gv[frames:frames + 2, lo:hi] = jnp.zeros((2, 2, width, chans), BF16)

        act_grads(frames - 2, lo, hi)
        pre_grads(groups - 1, lo, hi)
        if p == pairs - 1:
            send_edges(groups - 1)
        temporal_term(groups - 1, lo, hi, groups == 1 and p == 0)
        spatial_term(groups - 1, p, groups == 1 and p == 0)

    def put(tap, value):
        if not scatter:
            wg[tap * chans:(tap + 1) * chans] = value
            return
        blocks = part.shape[2]
        for n in range(chans // 16):
            at = tap * (chans // 16) + n
            owner = at // blocks
            part[owner // 2, owner % 2, at % blocks] = value[n * 16:(n + 1) * 16]

    for i in range(3):
        for j in range(3):
            spot = pl.ds(j * chans, chans)
            put(i * 3 + j, acc[i, spot, 0:chans] + acc[i + 1, spot, chans:2 * chans])
    for k in range(3):
        total = None
        for a in range(2):
            piece = tacc[a * chans:(a + 1) * chans, (a + k) * chans:(a + k + 1) * chans]
            total = piece if total is None else total + piece
        put(9 + k, total)

    if scatter:
        core_copy = remote(part.at[:, 1 - core], r1, s1s, s1r, {"row": me_r + 1 - 2 * core})
        core_copy.start()

    if scatter:
        core_copy.wait_recv()

        def narrow(q, carry):
            s1[q % plane, q // plane] = (part[q, core] + r1[q]).astype(BF16)
            return carry

        lax.fori_loop(0, chips, narrow, 0)

        def in_plane(o):
            p = (me_p + o) % plane
            return remote(s1.at[p], r2.at[me_p], s2s.at[o], s2r.at[me_p], chip(p))

        for o in range(1, plane):
            in_plane(o).start()

    outs.append(backward(groups - 1))

    if scatter:
        for o in range(1, plane):
            p = (me_p + plane - o) % plane
            remote(s1.at[p], r2.at[p], s2s.at[o], s2r.at[p], chip(p)).wait_recv()

        def gather(d, carry):
            total = part[d * plane + me_p, core] + r1[d * plane + me_p]
            for o in range(1, plane):
                total = total + r2[(me_p + plane - o) % plane, d].astype(F32)
            s3[d] = total
            return carry

        lax.fori_loop(0, nd, gather, 0)

        def along_dp(o):
            d = (me_d + o) % nd
            return remote(s3.at[d], r3.at[me_d], s3s.at[o], s3r.at[me_d], {"dp": d})

        for o in range(1, nd):
            along_dp(o).start()

    @pl.when(has_prev)
    def _():
        a_next.wait_recv()

    @pl.when(jnp.logical_not(has_prev))
    def _():
        ax[0:2] = jnp.zeros((2, rows, width, chans), BF16)

    outs.append(mix(0))

    if scatter:
        wg[...] = s3[me_d].reshape(wg.shape)
        for o in range(1, nd):
            d = (me_d + nd - o) % nd
            remote(s3.at[d], r3.at[d], s3s.at[o], s3r.at[d], {"dp": d}).wait_recv()
            wg[...] += r3[d].reshape(wg.shape)
            along_dp(o).wait_send()
        wg[...] = wg[...] * scale
        for o in range(1, plane):
            in_plane(o).wait_send()
        core_copy.wait_send()

    pl.when(has_up)(x_up.wait_send)
    pl.when(has_down)(x_down.wait_send)
    for copy in g_prev:
        pl.when(has_prev)(copy.wait_send)
    pl.when(has_next)(a_next.wait_send)
    for h in range(groups):
        pl.when(has_up)(p_up[h].wait_send)
        pl.when(has_down)(p_down[h].wait_send)
    for copy in outs:
        copy.wait()


def on_device(sizes, clip_input, cotangent, spatial_weight, temporal_weight):
    x, g = clip_input[0], cotangent[0]
    frames, rows, width, chans = x.shape
    nd, nf, nr = sizes
    devices = nd * nf * nr
    scale = 1.0 / math.sqrt(nd * frames * nf * rows * nr * width)
    terms = 12 * chans
    own = terms // devices
    scatter = own % 16 == 0 and terms % devices == 0 and nr % 2 == 0
    chips = devices // 2
    blocks = own // 16
    dma, regular = pltpu.SemaphoreType.DMA, pltpu.VMEM
    scratch = [
        regular((frames, rows, width, chans), BF16),
        regular((2, frames, width, chans), BF16),
        regular((frames, rows + 2, width, 3 * chans), BF16),
        regular((frames + 2, rows, width, chans), BF16),
        regular((frames + 2, rows, width, chans), BF16),
        regular((frames, rows, width, chans), F32),
        regular((frames, rows, width, chans), BF16),
        regular((frames, rows + 2, width, 3 * chans), BF16),
        regular((2, frames, width, chans), BF16),
        regular((2, frames, width, chans), BF16),
        regular((12 * chans, 2 * chans), BF16),
        regular((12 * chans, 2 * chans), BF16),
        regular((4 * chans, 2 * chans), BF16),
        regular((4 * chans, 2 * chans), BF16),
        regular((4, 3 * chans, 2 * chans), F32),
        regular((2 * chans, 4 * chans), F32),
    ]
    if scatter:
        scratch += [
            regular((chips, 2, blocks, 16, chans), F32),
            regular((chips, blocks, 16, chans), F32),
            regular((chips // nd, nd, blocks, 16, chans), BF16),
            regular((chips // nd, nd, blocks, 16, chans), BF16),
            regular((nd, blocks, 16, chans), F32),
            regular((nd, blocks, 16, chans), F32),
        ]
    scratch += [
        regular((frames, rows, width, chans), BF16),
        regular((frames, rows, width, chans), BF16),
        dma((2,)), dma((frames,)),
        dma((2,)), dma((2,)), dma((rows // 2,)), dma((rows // 2,)), dma, dma,
        dma((2, frames // 2)), dma((2, frames // 2)),
    ]
    if scatter:
        scratch += [dma, dma, dma((chips // nd,)), dma((chips // nd,)), dma((nd,)), dma((nd,))]

    def kernel(*refs):
        refs = list(refs)
        if not scatter:
            refs[23:23] = [None] * 6
            refs += [None] * 6
        block_kernel(sizes, scale, *refs)

    whole = jax.ShapeDtypeStruct(x.shape, BF16)
    grads = jax.ShapeDtypeStruct((own if scatter else terms, chans), F32)
    anywhere = pl.BlockSpec(memory_space=pl.ANY)
    vmem = pl.BlockSpec(memory_space=pltpu.VMEM)
    y, dx, wg = pl.pallas_call(
        kernel,
        out_shape=(whole, whole, grads),
        in_specs=[anywhere, anywhere, vmem, vmem],
        out_specs=(anywhere, anywhere, vmem),
        scratch_shapes=scratch,
        compiler_params=pltpu.CompilerParams(
            collective_id=0, has_side_effects=True, vmem_limit_bytes=56 * 1024 * 1024
        ),
    )(x, g, spatial_weight, temporal_weight)
    if not scatter:
        wg = scale * lax.psum_scatter(
            wg, ("dp", "frame", "row"), scatter_dimension=0, tiled=True
        )
    return (y[None], dx[None], wg)


def solution(mesh):
    spread = P("dp", "frame", "row", None, None)
    sizes = tuple(mesh.shape[name] for name in ("dp", "frame", "row"))
    return jax.shard_map(
        functools.partial(on_device, sizes),
        mesh=mesh,
        in_specs=(spread, spread, P(), P()),
        out_specs=(spread, spread, P(("dp", "frame", "row"), None)),
        check_vma=False,
    )
```
